32 devices in a mesh: feat: 8 (over y, x, core), samp: 4 (over z).
Axes of the slice: x: 2, y: 2, z: 4, core: 2. Of those that a mesh axis runs over, the one named last changes fastest.
Arguments:
- hash_codes: int32 [8, 3072, 1024], P('feat', 'samp'), may hold values from 0 to 4095
- sample_index: int32 [8, 8192], P('feat', 'samp'), may hold values from 0 to 767, as said below
- labels: int32 [2048, 4], P('feat', 'samp'), may hold values 0 or 1
- encoder_first: bfloat16 [8, 1024, 2048], P('feat'), may hold values from -0.1875 to 0.1875
- encoder_second: bfloat16 [8, 2048, 256], P('feat'), may hold values from -0.125 to 0.125
- top_weight: bfloat16 [64, 1024], replicated, may hold values from -0.75 to 0.75
- score_vector: bfloat16 [1024], replicated, may hold values from -0.1875 to 0.1875
Outputs:
- row_grads: float32 [8, 3072, 256], P('feat', 'samp')
- grad_first: float32 [8, 1024, 2048], P('feat', 'samp')
- grad_second: float32 [8, 2048, 256], P('feat', 'samp')
The draws below stay inside these ranges and needn't reach their ends.
Inputs may be any that keep to these rules, and one draw needn't show every extreme that they name: `sample_index`: for each feature and sample group the slots used by the group's 2048 samples are 0 to some count minus 1, each at least once; for some feature and group that count is 768.
All inputs are finite; a program needn't handle non-finite values. No bound on the sum of `labels` on one device may be relied on, other than what follows from the above.
Results may differ from the reference program's by a relative error of at most 0.019.
Values may be sent and summed in bfloat16 or wider, within the bound.
A program may use at most 128 MiB of HBM per device.

```python
import jax
import jax.numpy as jnp
from jax import lax

HASHES = 1024
HID1 = 2048
EMB = 256
HID = 1024
BUCKETS = 4096
ROWS_DEV = 768
SB_DEV = 256
FEATS = 8
GROUPS = 4
GROUP = 2048
N_FEAT = 8
N_SAMP = 4


def draw_sample_index(key, part):
    group = SB_DEV * N_FEAT
    lanes = FEATS * N_SAMP
    key_count, key_pick, key_order, key_fill = jax.random.split(key, 4)
    counts = jax.random.randint(key_count, (lanes,), ROWS_DEV // 4, ROWS_DEV + 1)
    chosen = jax.random.randint(key_pick, (), 0, lanes)
    counts = jnp.where(jnp.arange(lanes) == chosen, ROWS_DEV, counts).astype(jnp.int32)
    scores = jax.random.randint(key_order, (lanes, group), 0, 2 ** 30 // group) * group + jnp.arange(group)[None, :]
    ordering = jnp.argsort(scores, axis=1).astype(jnp.int32)
    filler = jax.random.randint(key_fill, (lanes, group), 0, 2 ** 20)
    result = jnp.where(ordering < counts[:, None], ordering, filler % counts[:, None])
    return result.astype(jnp.int32).reshape(FEATS, N_SAMP * group)


def plant(entries, own_key, smallest, high):
    longest = entries.shape.index(max(entries.shape))
    spots = []
    for shift in (0, 1):
        where = [jax.random.randint(jax.random.fold_in(own_key, axis), (), 0, length) for axis, length in enumerate(entries.shape)]
        where[longest] = (where[longest] + shift) % entries.shape[longest]
        spots.append(tuple(where))
    return entries.at[spots[0]].set(smallest).at[spots[1]].set(high)


def block_levels(stream_key, shape, shards, least, largest):
    def one(axis_at, blocks):
        steps = jax.random.uniform(jax.random.fold_in(jax.random.fold_in(stream_key, 6), axis_at), (blocks,), jnp.float32, least / len(shards), largest / len(shards))
        return jnp.repeat(jnp.exp(steps), shape[axis_at] // blocks).reshape((-1,) + (1,) * (len(shape) - axis_at - 1))

    factor_of = one(*shards[0])
    for cut in shards[1:]:
        factor_of = factor_of * one(*cut)
    return factor_of


def bell_draw(own_key, extent, spread, reach, shards=(), kind=jnp.bfloat16):
    level = block_levels(own_key, extent, shards, -0.22, 0.18) if shards else 1.0
    values = jax.random.normal(own_key, extent, jnp.float32) * spread * level
    return jnp.minimum(jnp.maximum(values, -reach), reach).astype(kind)


def setup_inputs(seed: int = 0) -> dict:
    key_list = jax.random.split(jax.random.key(seed), 8)
    return {
        "hash_codes": plant(jax.random.randint(key_list[0], (FEATS, GROUPS * ROWS_DEV, HASHES), 0, BUCKETS), jax.random.fold_in(key_list[0], 1), 0, BUCKETS - 1).astype(jnp.int32),
        "sample_index": draw_sample_index(jax.random.fold_in(key_list[7], 71), 0),
        "labels": plant((jax.random.randint(key_list[2], (GROUP, GROUPS), 0, 2) < 1).astype(jnp.int32), jax.random.fold_in(key_list[2], 1), 0, 1),
        "encoder_first": bell_draw(key_list[3], (FEATS, HASHES, HID1), HASHES ** -0.5, 0.1875, ((0, 8),)),
        "encoder_second": bell_draw(key_list[4], (FEATS, HID1, EMB), HID1 ** -0.5, 0.125, ((0, 8),)),
        "top_weight": bell_draw(key_list[5], (FEATS * FEATS, HID), (FEATS * FEATS) ** -0.5, 0.75),
        "score_vector": bell_draw(key_list[6], (HID,), HID ** -0.5, 0.1875),
    }


loss_scale = 256.0


def silu_slope(inputs):
    logistic = jax.nn.sigmoid(inputs)
    return logistic * (1.0 + inputs * (1.0 - logistic))


def encode_codes(codes_block):
    return (codes_block.astype(jnp.float32) * (2.0 / (BUCKETS - 1)) - 1.0).astype(jnp.bfloat16)


def take_rows(row_table, positions):
    return jnp.take(row_table, positions, axis=0)


def sum_rows(emb_delta, positions):
    return jax.ops.segment_sum(emb_delta.astype(jnp.float32), positions, num_segments=ROWS_DEV)


def top_tower(picked, label_block, top_weight, score_vector):
    feats, count, width = picked.shape
    picked_float = picked.astype(jnp.float32)
    weight_float = top_weight.astype(jnp.float32)
    pair_dots = (jnp.einsum("fne,hne->nfh", picked_float, picked_float) * (width ** -0.5)).astype(jnp.bfloat16)
    pair_flat = pair_dots.reshape(count, feats * feats)
    top_pre = jnp.dot(pair_flat, top_weight, preferred_element_type=jnp.float32)
    top_hidden = jax.nn.silu(top_pre).astype(jnp.bfloat16)
    logits = jnp.dot(top_hidden, score_vector, preferred_element_type=jnp.float32)
    dlogit = loss_scale * (jax.nn.sigmoid(logits) - label_block.astype(jnp.float32))
    top_delta = (dlogit[:, None] * score_vector.astype(jnp.float32)[None, :] * silu_slope(top_pre)).astype(jnp.bfloat16)
    pair_delta = jnp.einsum("nk,jk->nj", top_delta.astype(jnp.float32), weight_float).reshape(count, feats, feats)
    pair_sym = (pair_delta + jnp.swapaxes(pair_delta, 1, 2)).astype(jnp.bfloat16)
    emb_delta = jnp.einsum("nfh,hne->fne", pair_sym.astype(jnp.float32), picked_float) * (width ** -0.5)
    return emb_delta.astype(jnp.bfloat16)


def reference(hash_codes, sample_index, labels, encoder_first, encoder_second, top_weight, score_vector):
    group = SB_DEV * N_FEAT
    first_float = encoder_first.astype(jnp.float32)
    second_float = encoder_second.astype(jnp.float32)
    grad_first = jnp.zeros(encoder_first.shape, jnp.float32)
    grad_second = jnp.zeros(encoder_second.shape, jnp.float32)
    row_parts = []
    for group_id in range(N_SAMP):
        encoded = encode_codes(hash_codes[:, group_id * ROWS_DEV:(group_id + 1) * ROWS_DEV])
        encoded_float = encoded.astype(jnp.float32)
        first_pre = jnp.einsum("frh,fhk->frk", encoded_float, first_float)
        first_hidden = jax.nn.silu(first_pre).astype(jnp.bfloat16)
        row_table = jnp.einsum("frk,fke->fre", first_hidden.astype(jnp.float32), second_float).astype(jnp.bfloat16)
        positions = sample_index[:, group_id * group:(group_id + 1) * group]
        picked = jax.vmap(take_rows)(row_table, positions)
        emb_delta = top_tower(picked, labels[:, group_id], top_weight, score_vector)
        row_grads = jax.vmap(sum_rows)(emb_delta, positions)
        row_parts.append(row_grads)
        row_delta = row_grads.astype(jnp.bfloat16).astype(jnp.float32)
        second_term = jnp.einsum("frk,fre->fke", first_hidden.astype(jnp.float32), row_delta)
        first_delta = (jnp.einsum("fre,fke->frk", row_delta, second_float) * silu_slope(first_pre)).astype(jnp.bfloat16)
        first_term = jnp.einsum("frh,frk->fhk", encoded_float, first_delta.astype(jnp.float32))
        grad_second = grad_second + lax.optimization_barrier(second_term.astype(jnp.bfloat16)).astype(jnp.float32)
        grad_first = grad_first + lax.optimization_barrier(first_term.astype(jnp.bfloat16)).astype(jnp.float32)
    return jnp.concatenate(row_parts, axis=1), grad_first, grad_second
```

```python
import jax
import jax.numpy as jnp
from jax import lax
from jax.sharding import PartitionSpec as P

BUCKETS = 4096


loss_scale = 256.0


def silu_slope(inputs):
    logistic = jax.nn.sigmoid(inputs)
    return logistic * (1.0 + inputs * (1.0 - logistic))


def top_tower(picked, label_block, top_weight, score_vector):
    feats, count, width = picked.shape
    pair_dots = (
        jnp.einsum("fne,hne->nfh", picked, picked, preferred_element_type=jnp.float32)
        * width ** (-0.5)
    ).astype(jnp.bfloat16)
    pair_flat = pair_dots.reshape(count, feats * feats)
    top_pre = jnp.dot(pair_flat, top_weight, preferred_element_type=jnp.float32)
    top_hidden = jax.nn.silu(top_pre).astype(jnp.bfloat16)
    logits = jnp.dot(top_hidden, score_vector, preferred_element_type=jnp.float32)
    dlogit = loss_scale * (jax.nn.sigmoid(logits) - label_block.astype(jnp.float32))
    top_delta = (
        dlogit[:, None] * score_vector.astype(jnp.float32)[None, :] * silu_slope(top_pre)
    ).astype(jnp.bfloat16)
    pair_delta = jnp.einsum(
        "nk,jk->nj", top_delta, top_weight, preferred_element_type=jnp.float32
    ).reshape(count, feats, feats)
    pair_sym = (pair_delta + jnp.swapaxes(pair_delta, 1, 2)).astype(jnp.bfloat16)
    emb_delta = jnp.einsum(
        "nfh,hne->fne", pair_sym, picked, preferred_element_type=jnp.float32
    ) * width ** (-0.5)
    return emb_delta.astype(jnp.bfloat16)


def local(
    hash_codes, sample_index, labels, encoder_first, encoder_second, top_weight, score_vector
):
    feat_count = lax.axis_size("feat")
    samp_count = lax.axis_size("samp")
    samp_at = lax.axis_index("samp")
    weight_first, weight_second = encoder_first[0], encoder_second[0]
    hash_count, hidden_count = weight_first.shape
    emb_width = weight_second.shape[1]
    encoded = (hash_codes[0].astype(jnp.float32) * (2.0 / (BUCKETS - 1)) - 1.0).astype(jnp.bfloat16)
    slot_count = encoded.shape[0]
    encoded_all = lax.all_gather(encoded, "samp", axis=0, tiled=True)
    first_pre = jnp.dot(encoded, weight_first, preferred_element_type=jnp.float32)
    first_hidden = jax.nn.silu(first_pre).astype(jnp.bfloat16)
    row_table = jnp.dot(first_hidden, weight_second, preferred_element_type=jnp.float32).astype(
        jnp.bfloat16
    )
    positions = sample_index[0]
    slots = lax.broadcasted_iota(jnp.int32, (positions.shape[0], slot_count), 1)
    chooser = (positions[:, None] == slots).astype(jnp.bfloat16)
    chosen_rows = (
        jnp.dot(chooser, row_table, preferred_element_type=jnp.float32)
        .astype(jnp.bfloat16)
        .reshape(feat_count, -1, emb_width)
    )
    picked = lax.all_to_all(chosen_rows, "feat", split_axis=0, concat_axis=0, tiled=True)
    emb_delta = top_tower(picked, labels[:, 0], top_weight, score_vector)
    returned = lax.all_to_all(emb_delta, "feat", split_axis=0, concat_axis=0, tiled=True)
    slots_back = lax.broadcasted_iota(jnp.int32, (slot_count, positions.shape[0]), 0)
    placer = (positions[None, :] == slots_back).astype(jnp.bfloat16)
    row_grads = jnp.dot(
        placer, returned.reshape(-1, emb_width), preferred_element_type=jnp.float32
    )
    row_delta_all = lax.all_gather(row_grads.astype(jnp.bfloat16), "samp", axis=0, tiled=True)

    slope_all = silu_slope(
        jnp.dot(encoded_all, weight_first, preferred_element_type=jnp.float32)
    ).astype(jnp.bfloat16)
    share = hidden_count // samp_count
    weight_share = lax.dynamic_slice_in_dim(weight_first, samp_at * share, share, axis=1)
    hidden_share = jax.nn.silu(
        jnp.dot(encoded_all, weight_share, preferred_element_type=jnp.float32)
    ).astype(jnp.bfloat16)
    depth = hash_count // samp_count
    encoded_share = lax.dynamic_slice_in_dim(encoded_all, samp_at * depth, depth, axis=1)
    share_second = jnp.einsum(
        "rk,re->ke", hidden_share, row_delta_all, preferred_element_type=jnp.float32
    )
    first_back = jnp.einsum(
        "re,ke->rk", row_delta_all, weight_second, preferred_element_type=jnp.float32
    )
    first_delta = (first_back * slope_all.astype(jnp.float32)).astype(jnp.bfloat16)
    share_first = jnp.einsum(
        "rh,rk->hk", encoded_share, first_delta, preferred_element_type=jnp.float32
    )
    return (row_grads[None], share_first[None], share_second[None])


def solution(mesh):
    return jax.shard_map(
        local,
        mesh=mesh,
        in_specs=(
            P("feat", "samp", None),
            P("feat", "samp"),
            P("feat", "samp"),
            P("feat", None, None),
            P("feat", None, None),
            P(),
            P(),
        ),
        out_specs=(P("feat", "samp", None), P("feat", "samp", None), P("feat", "samp", None)),
        check_vma=False,
    )
```

```python
import jax
import jax.numpy as jnp
from jax import lax
from jax.sharding import PartitionSpec as P

BUCKETS = 4096


loss_scale = 256.0


def silu_slope(inputs):
    logistic = jax.nn.sigmoid(inputs)
    return logistic * (1.0 + inputs * (1.0 - logistic))


def top_tower(picked, label_block, top_weight, score_vector):
    feats, count, width = picked.shape
    pair_dots = (
        jnp.einsum("fne,hne->nfh", picked, picked, preferred_element_type=jnp.float32)
        * width ** (-0.5)
    ).astype(jnp.bfloat16)
    pair_flat = pair_dots.reshape(count, feats * feats)
    top_pre = jnp.dot(pair_flat, top_weight, preferred_element_type=jnp.float32)
    top_hidden = jax.nn.silu(top_pre).astype(jnp.bfloat16)
    logits = jnp.dot(top_hidden, score_vector, preferred_element_type=jnp.float32)
    dlogit = loss_scale * (jax.nn.sigmoid(logits) - label_block.astype(jnp.float32))
    top_delta = (
        dlogit[:, None] * score_vector.astype(jnp.float32)[None, :] * silu_slope(top_pre)
    ).astype(jnp.bfloat16)
    pair_delta = jnp.einsum(
        "nk,jk->nj", top_delta, top_weight, preferred_element_type=jnp.float32
    ).reshape(count, feats, feats)
    pair_sym = (pair_delta + jnp.swapaxes(pair_delta, 1, 2)).astype(jnp.bfloat16)
    emb_delta = jnp.einsum(
        "nfh,hne->fne", pair_sym, picked, preferred_element_type=jnp.float32
    ) * width ** (-0.5)
    return emb_delta.astype(jnp.bfloat16)


def local(
    hash_codes, sample_index, labels, encoder_first, encoder_second, top_weight, score_vector
):
    feat_count = lax.axis_size("feat")
    samp_count = lax.axis_size("samp")
    samp_at = lax.axis_index("samp")
    half = samp_count // 2
    across = [(i, i // 2 * 2 + (i + 1) % 2) for i in range(samp_count)]
    weight_first, weight_second = encoder_first[0], encoder_second[0]
    hash_count, hidden_count = weight_first.shape
    emb_width = weight_second.shape[1]
    encoded = (hash_codes[0].astype(jnp.float32) * (2.0 / (BUCKETS - 1)) - 1.0).astype(jnp.bfloat16)
    slot_count = encoded.shape[0]
    encoded = lax.optimization_barrier(encoded)
    encoded_far = lax.ppermute(encoded, "samp", across)
    first_pre = jnp.dot(encoded, weight_first, preferred_element_type=jnp.float32)
    first_hidden = jax.nn.silu(first_pre).astype(jnp.bfloat16)
    slope = silu_slope(first_pre).astype(jnp.bfloat16)
    row_table = jnp.dot(first_hidden, weight_second, preferred_element_type=jnp.float32).astype(
        jnp.bfloat16
    )
    positions = sample_index[0]
    slots = lax.broadcasted_iota(jnp.int32, (positions.shape[0], slot_count), 1)
    chooser = (positions[:, None] == slots).astype(jnp.bfloat16)
    chosen_rows = (
        jnp.dot(chooser, row_table, preferred_element_type=jnp.float32)
        .astype(jnp.bfloat16)
        .reshape(feat_count, -1, emb_width)
    )
    picked = lax.all_to_all(chosen_rows, "feat", split_axis=0, concat_axis=0, tiled=True)
    emb_delta = top_tower(picked, labels[:, 0], top_weight, score_vector)
    emb_delta, slope, first_hidden = lax.optimization_barrier((emb_delta, slope, first_hidden))
    returned = lax.all_to_all(emb_delta, "feat", split_axis=0, concat_axis=0, tiled=True)
    slots_back = lax.broadcasted_iota(jnp.int32, (slot_count, positions.shape[0]), 0)
    placer = (positions[None, :] == slots_back).astype(jnp.bfloat16)
    row_grads = jnp.dot(
        placer, returned.reshape(-1, emb_width), preferred_element_type=jnp.float32
    )
    row_delta = row_grads.astype(jnp.bfloat16)
    row_delta_far = lax.ppermute(row_delta, "samp", across)

    first_pre_far = jnp.dot(encoded_far, weight_first, preferred_element_type=jnp.float32)
    hidden_far, slope_far = lax.optimization_barrier(
        (
            jax.nn.silu(first_pre_far).astype(jnp.bfloat16),
            silu_slope(first_pre_far).astype(jnp.bfloat16),
        )
    )

    def delta_of(rows, factor):
        back = jnp.einsum("re,ke->rk", rows, weight_second, preferred_element_type=jnp.float32)
        return (back * factor.astype(jnp.float32)).astype(jnp.bfloat16)

    near = (encoded, first_hidden, row_delta, delta_of(row_delta, slope))
    far = (encoded_far, hidden_far, row_delta_far, delta_of(row_delta_far, slope_far))
    depth = hash_count // samp_count
    share = hidden_count // samp_count

    def first_part(group, at):
        columns = lax.dynamic_slice_in_dim(group[0], at * depth, depth, axis=1)
        return jnp.einsum("rh,rk->hk", columns, group[3], preferred_element_type=jnp.float32)

    def second_part(group, at):
        columns = lax.dynamic_slice_in_dim(group[1], at * share, share, axis=1)
        return jnp.einsum("rk,re->ke", columns, group[2], preferred_element_type=jnp.float32)

    firsts, seconds = [], []
    for step in range(1, half):
        target = (samp_at + 2 * step) % samp_count
        pairs = [(i, (i + 2 * step) % samp_count) for i in range(samp_count)]
        first_out = (first_part(near, target) + first_part(far, target)).astype(jnp.bfloat16)
        firsts.append(lax.ppermute(first_out, "samp", pairs))
        second_out = (second_part(near, target) + second_part(far, target)).astype(jnp.bfloat16)
        seconds.append(lax.ppermute(second_out, "samp", pairs))
    share_first = first_part(near, samp_at) + first_part(far, samp_at)
    share_second = second_part(near, samp_at) + second_part(far, samp_at)
    for arrived in firsts:
        share_first = share_first + arrived.astype(jnp.float32)
    for arrived in seconds:
        share_second = share_second + arrived.astype(jnp.float32)
    return (row_grads[None], share_first[None], share_second[None])


def solution(mesh):
    return jax.shard_map(
        local,
        mesh=mesh,
        in_specs=(
            P("feat", "samp", None),
            P("feat", "samp"),
            P("feat", "samp"),
            P("feat", None, None),
            P("feat", None, None),
            P(),
            P(),
        ),
        out_specs=(P("feat", "samp", None), P("feat", "samp", None), P("feat", "samp", None)),
        check_vma=False,
    )
```

```python
import jax
import jax.numpy as jnp
from jax import lax
from jax.sharding import PartitionSpec as P

BUCKETS = 4096


loss_scale = 256.0


def silu_slope(inputs):
    logistic = jax.nn.sigmoid(inputs)
    return logistic * (1.0 + inputs * (1.0 - logistic))


def top_tower(picked, label_block, top_weight, score_vector):
    feats, count, width = picked.shape
    pair_dots = (
        jnp.einsum("fne,hne->nfh", picked, picked, preferred_element_type=jnp.float32)
        * width ** (-0.5)
    ).astype(jnp.bfloat16)
    pair_flat = pair_dots.reshape(count, feats * feats)
    top_pre = jnp.dot(pair_flat, top_weight, preferred_element_type=jnp.float32)
    top_hidden = jax.nn.silu(top_pre).astype(jnp.bfloat16)
    logits = jnp.dot(top_hidden, score_vector, preferred_element_type=jnp.float32)
    dlogit = loss_scale * (jax.nn.sigmoid(logits) - label_block.astype(jnp.float32))
    top_delta = (
        dlogit[:, None] * score_vector.astype(jnp.float32)[None, :] * silu_slope(top_pre)
    ).astype(jnp.bfloat16)
    pair_delta = jnp.einsum(
        "nk,jk->nj", top_delta, top_weight, preferred_element_type=jnp.float32
    ).reshape(count, feats, feats)
    pair_sym = (pair_delta + jnp.swapaxes(pair_delta, 1, 2)).astype(jnp.bfloat16)
    emb_delta = jnp.einsum(
        "nfh,hne->fne", pair_sym, picked, preferred_element_type=jnp.float32
    ) * width ** (-0.5)
    return emb_delta.astype(jnp.bfloat16)


def local(
    hash_codes, sample_index, labels, encoder_first, encoder_second, top_weight, score_vector
):
    feat_count = lax.axis_size("feat")
    samp_count = lax.axis_size("samp")
    samp_at = lax.axis_index("samp")
    half = samp_count // 2
    across = [(i, i // 2 * 2 + (i + 1) % 2) for i in range(samp_count)]
    weight_first, weight_second = encoder_first[0], encoder_second[0]
    hash_count, hidden_count = weight_first.shape
    emb_width = weight_second.shape[1]
    encoded = (hash_codes[0].astype(jnp.float32) * (2.0 / (BUCKETS - 1)) - 1.0).astype(jnp.bfloat16)
    slot_count = encoded.shape[0]
    encoded = lax.optimization_barrier(encoded)
    encoded_far = lax.ppermute(encoded, "samp", across)

    def hidden_of(codes):
        first_pre = jnp.dot(codes, weight_first, preferred_element_type=jnp.float32)
        return jax.nn.silu(first_pre).astype(jnp.bfloat16), silu_slope(first_pre).astype(jnp.bfloat16)

    row_table = lax.optimization_barrier(
        jnp.dot(
            hidden_of(encoded)[0], weight_second, preferred_element_type=jnp.float32
        ).astype(jnp.bfloat16)
    )
    positions = sample_index[0]
    slots = lax.broadcasted_iota(jnp.int32, (positions.shape[0], slot_count), 1)
    chooser = (positions[:, None] == slots).astype(jnp.bfloat16)
    chosen_rows = (
        jnp.dot(chooser, row_table, preferred_element_type=jnp.float32)
        .astype(jnp.bfloat16)
        .reshape(feat_count, -1, emb_width)
    )
    chosen_rows, encoded = lax.optimization_barrier((chosen_rows, encoded))
    first_hidden, slope = hidden_of(encoded)
    picked = lax.all_to_all(chosen_rows, "feat", split_axis=0, concat_axis=0, tiled=True)
    picked, encoded_far, slope, first_hidden = lax.optimization_barrier(
        (picked, encoded_far, slope, first_hidden)
    )
    emb_delta = top_tower(picked, labels[:, 0], top_weight, score_vector)
    returned = lax.all_to_all(emb_delta, "feat", split_axis=0, concat_axis=0, tiled=True)
    slots_back = lax.broadcasted_iota(jnp.int32, (slot_count, positions.shape[0]), 0)
    placer = (positions[None, :] == slots_back).astype(jnp.bfloat16)
    row_grads = jnp.dot(
        placer, returned.reshape(-1, emb_width), preferred_element_type=jnp.float32
    )
    row_delta = row_grads.astype(jnp.bfloat16)
    row_delta_far = lax.ppermute(row_delta, "samp", across)

    first_pre_far = jnp.dot(encoded_far, weight_first, preferred_element_type=jnp.float32)
    hidden_far, slope_far = lax.optimization_barrier(
        (
            jax.nn.silu(first_pre_far).astype(jnp.bfloat16),
            silu_slope(first_pre_far).astype(jnp.bfloat16),
        )
    )

    def delta_of(rows, factor):
        back = jnp.einsum("re,ke->rk", rows, weight_second, preferred_element_type=jnp.float32)
        return (back * factor.astype(jnp.float32)).astype(jnp.bfloat16)

    near = (encoded, first_hidden, row_delta, delta_of(row_delta, slope))
    far = (encoded_far, hidden_far, row_delta_far, delta_of(row_delta_far, slope_far))
    depth = hash_count // samp_count
    share = hidden_count // samp_count

    def first_part(group, at):
        columns = lax.dynamic_slice_in_dim(group[0], at * depth, depth, axis=1)
        return jnp.einsum("rh,rk->hk", columns, group[3], preferred_element_type=jnp.float32)

    def second_part(group, at):
        columns = lax.dynamic_slice_in_dim(group[1], at * share, share, axis=1)
        return jnp.einsum("rk,re->ke", columns, group[2], preferred_element_type=jnp.float32)

    firsts, seconds = [], []
    for step in range(1, half):
        target = (samp_at + 2 * step) % samp_count
        pairs = [(i, (i + 2 * step) % samp_count) for i in range(samp_count)]
        first_out = (first_part(near, target) + first_part(far, target)).astype(jnp.bfloat16)
        firsts.append(lax.ppermute(first_out, "samp", pairs))
        second_out = (second_part(near, target) + second_part(far, target)).astype(jnp.bfloat16)
        seconds.append(lax.ppermute(second_out, "samp", pairs))
    share_first = first_part(near, samp_at) + first_part(far, samp_at)
    share_second = second_part(near, samp_at) + second_part(far, samp_at)
    for arrived in firsts:
        share_first = share_first + arrived.astype(jnp.float32)
    for arrived in seconds:
        share_second = share_second + arrived.astype(jnp.float32)
    return (row_grads[None], share_first[None], share_second[None])


def solution(mesh):
    return jax.shard_map(
        local,
        mesh=mesh,
        in_specs=(
            P("feat", "samp", None),
            P("feat", "samp"),
            P("feat", "samp"),
            P("feat", None, None),
            P("feat", None, None),
            P(),
            P(),
        ),
        out_specs=(P("feat", "samp", None), P("feat", "samp", None), P("feat", "samp", None)),
        check_vma=False,
    )
```

```python
import jax
import jax.numpy as jnp
from jax import lax
from jax.sharding import PartitionSpec as P

BUCKETS = 4096


loss_scale = 256.0


def silu_slope(inputs):
    logistic = jax.nn.sigmoid(inputs)
    return logistic * (1.0 + inputs * (1.0 - logistic))


def top_tower(picked, label_block, top_weight, score_vector):
    feats, count, width = picked.shape
    pair_dots = (
        jnp.einsum("fne,hne->nfh", picked, picked, preferred_element_type=jnp.float32)
        * width ** (-0.5)
    ).astype(jnp.bfloat16)
    pair_flat = pair_dots.reshape(count, feats * feats)
    top_pre = jnp.dot(pair_flat, top_weight, preferred_element_type=jnp.float32)
    top_hidden = jax.nn.silu(top_pre).astype(jnp.bfloat16)
    logits = jnp.dot(top_hidden, score_vector, preferred_element_type=jnp.float32)
    dlogit = loss_scale * (jax.nn.sigmoid(logits) - label_block.astype(jnp.float32))
    top_delta = (
        dlogit[:, None] * score_vector.astype(jnp.float32)[None, :] * silu_slope(top_pre)
    ).astype(jnp.bfloat16)
    pair_delta = jnp.einsum(
        "nk,jk->nj", top_delta, top_weight, preferred_element_type=jnp.float32
    ).reshape(count, feats, feats)
    pair_sym = (pair_delta + jnp.swapaxes(pair_delta, 1, 2)).astype(jnp.bfloat16)
    emb_delta = jnp.einsum(
        "nfh,hne->fne", pair_sym, picked, preferred_element_type=jnp.float32
    ) * width ** (-0.5)
    return emb_delta.astype(jnp.bfloat16)


def local(
    hash_codes, sample_index, labels, encoder_first, encoder_second, top_weight, score_vector
):
    feat_count = lax.axis_size("feat")
    samp_count = lax.axis_size("samp")
    samp_at = lax.axis_index("samp")
    half = samp_count // 2
    across = [(i, i // 2 * 2 + (i + 1) % 2) for i in range(samp_count)]
    weight_first, weight_second = encoder_first[0], encoder_second[0]
    hash_count, hidden_count = weight_first.shape
    emb_width = weight_second.shape[1]
    encoded = (hash_codes[0].astype(jnp.float32) * (2.0 / (BUCKETS - 1)) - 1.0).astype(jnp.bfloat16)
    slot_count = encoded.shape[0]
    encoded = lax.optimization_barrier(encoded)
    encoded_far = lax.ppermute(encoded, "samp", across)

    def hidden_of(codes):
        first_pre = jnp.dot(codes, weight_first, preferred_element_type=jnp.float32)
        return jax.nn.silu(first_pre).astype(jnp.bfloat16), silu_slope(first_pre).astype(jnp.bfloat16)

    row_table = lax.optimization_barrier(
        jnp.dot(
            hidden_of(encoded)[0], weight_second, preferred_element_type=jnp.float32
        ).astype(jnp.bfloat16)
    )
    positions = sample_index[0]
    slots = lax.broadcasted_iota(jnp.int32, (positions.shape[0], slot_count), 1)
    chooser = (positions[:, None] == slots).astype(jnp.bfloat16)
    chosen_rows = (
        jnp.dot(chooser, row_table, preferred_element_type=jnp.float32)
        .astype(jnp.bfloat16)
        .reshape(feat_count, -1, emb_width)
    )
    chosen_rows, encoded = lax.optimization_barrier((chosen_rows, encoded))
    first_hidden, slope = hidden_of(encoded)
    picked = lax.all_to_all(chosen_rows, "feat", split_axis=0, concat_axis=0, tiled=True)
    picked, slope, first_hidden = lax.optimization_barrier((picked, slope, first_hidden))
    emb_delta = top_tower(picked, labels[:, 0], top_weight, score_vector)
    emb_delta, encoded_far = lax.optimization_barrier((emb_delta, encoded_far))
    returned = lax.all_to_all(emb_delta, "feat", split_axis=0, concat_axis=0, tiled=True)
    slots_back = lax.broadcasted_iota(jnp.int32, (slot_count, positions.shape[0]), 0)
    placer = (positions[None, :] == slots_back).astype(jnp.bfloat16)
    row_grads = jnp.dot(
        placer, returned.reshape(-1, emb_width), preferred_element_type=jnp.float32
    )
    row_delta = row_grads.astype(jnp.bfloat16)
    row_delta_far = lax.ppermute(row_delta, "samp", across)

    first_pre_far = jnp.dot(encoded_far, weight_first, preferred_element_type=jnp.float32)
    hidden_far, slope_far = lax.optimization_barrier(
        (
            jax.nn.silu(first_pre_far).astype(jnp.bfloat16),
            silu_slope(first_pre_far).astype(jnp.bfloat16),
        )
    )

    def delta_of(rows, factor):
        back = jnp.einsum("re,ke->rk", rows, weight_second, preferred_element_type=jnp.float32)
        return (back * factor.astype(jnp.float32)).astype(jnp.bfloat16)

    near = (encoded, first_hidden, row_delta, delta_of(row_delta, slope))
    far = (encoded_far, hidden_far, row_delta_far, delta_of(row_delta_far, slope_far))
    depth = hash_count // samp_count
    share = hidden_count // samp_count

    def first_part(group, at):
        columns = lax.dynamic_slice_in_dim(group[0], at * depth, depth, axis=1)
        return jnp.einsum("rh,rk->hk", columns, group[3], preferred_element_type=jnp.float32)

    def second_part(group, at):
        columns = lax.dynamic_slice_in_dim(group[1], at * share, share, axis=1)
        return jnp.einsum("rk,re->ke", columns, group[2], preferred_element_type=jnp.float32)

    firsts, seconds = [], []
    for step in range(1, half):
        target = (samp_at + 2 * step) % samp_count
        pairs = [(i, (i + 2 * step) % samp_count) for i in range(samp_count)]
        first_out = (first_part(near, target) + first_part(far, target)).astype(jnp.bfloat16)
        firsts.append(lax.ppermute(first_out, "samp", pairs))
        second_out = (second_part(near, target) + second_part(far, target)).astype(jnp.bfloat16)
        seconds.append(lax.ppermute(second_out, "samp", pairs))
    share_first = first_part(near, samp_at) + first_part(far, samp_at)
    share_second = second_part(near, samp_at) + second_part(far, samp_at)
    for arrived in firsts:
        share_first = share_first + arrived.astype(jnp.float32)
    for arrived in seconds:
        share_second = share_second + arrived.astype(jnp.float32)
    return (row_grads[None], share_first[None], share_second[None])


def solution(mesh):
    return jax.shard_map(
        local,
        mesh=mesh,
        in_specs=(
            P("feat", "samp", None),
            P("feat", "samp"),
            P("feat", "samp"),
            P("feat", None, None),
            P("feat", None, None),
            P(),
            P(),
        ),
        out_specs=(P("feat", "samp", None), P("feat", "samp", None), P("feat", "samp", None)),
        check_vma=False,
    )
```

```python
import jax
import jax.numpy as jnp
from jax import lax
from jax.sharding import PartitionSpec as P

BUCKETS = 4096


loss_scale = 256.0


def silu_slope(inputs):
    logistic = jax.nn.sigmoid(inputs)
    return logistic * (1.0 + inputs * (1.0 - logistic))


def top_tower(picked, label_block, top_weight, score_vector):
    feats, count, width = picked.shape
    pair_dots = (
        jnp.einsum("fne,hne->nfh", picked, picked, preferred_element_type=jnp.float32)
        * width ** (-0.5)
    ).astype(jnp.bfloat16)
    pair_flat = pair_dots.reshape(count, feats * feats)
    top_pre = jnp.dot(pair_flat, top_weight, preferred_element_type=jnp.float32)
    top_hidden = jax.nn.silu(top_pre).astype(jnp.bfloat16)
    logits = jnp.dot(top_hidden, score_vector, preferred_element_type=jnp.float32)
    dlogit = loss_scale * (jax.nn.sigmoid(logits) - label_block.astype(jnp.float32))
    top_delta = (
        dlogit[:, None] * score_vector.astype(jnp.float32)[None, :] * silu_slope(top_pre)
    ).astype(jnp.bfloat16)
    pair_delta = jnp.einsum(
        "nk,jk->nj", top_delta, top_weight, preferred_element_type=jnp.float32
    ).reshape(count, feats, feats)
    pair_sym = (pair_delta + jnp.swapaxes(pair_delta, 1, 2)).astype(jnp.bfloat16)
    emb_delta = jnp.einsum(
        "nfh,hne->fne", pair_sym, picked, preferred_element_type=jnp.float32
    ) * width ** (-0.5)
    return emb_delta.astype(jnp.bfloat16)


def local(
    hash_codes, sample_index, labels, encoder_first, encoder_second, top_weight, score_vector
):
    feat_count = lax.axis_size("feat")
    samp_count = lax.axis_size("samp")
    samp_at = lax.axis_index("samp")
    half = samp_count // 2
    across = [(i, i // 2 * 2 + (i + 1) % 2) for i in range(samp_count)]
    weight_first, weight_second = encoder_first[0], encoder_second[0]
    hash_count, hidden_count = weight_first.shape
    emb_width = weight_second.shape[1]
    encoded = (hash_codes[0].astype(jnp.float32) * (2.0 / (BUCKETS - 1)) - 1.0).astype(jnp.bfloat16)
    slot_count = encoded.shape[0]
    encoded = lax.optimization_barrier(encoded)
    encoded_far = lax.ppermute(encoded, "samp", across)

    def hidden_of(codes):
        first_pre = jnp.dot(codes, weight_first, preferred_element_type=jnp.float32)
        return jax.nn.silu(first_pre).astype(jnp.bfloat16), silu_slope(first_pre).astype(jnp.bfloat16)

    row_table = lax.optimization_barrier(
        jnp.dot(
            hidden_of(encoded)[0], weight_second, preferred_element_type=jnp.float32
        ).astype(jnp.bfloat16)
    )
    positions = sample_index[0]
    slots = lax.broadcasted_iota(jnp.int32, (positions.shape[0], slot_count), 1)
    chooser = (positions[:, None] == slots).astype(jnp.bfloat16)
    chosen_rows = (
        jnp.dot(chooser, row_table, preferred_element_type=jnp.float32)
        .astype(jnp.bfloat16)
        .reshape(feat_count, -1, emb_width)
    )
    chosen_rows, encoded = lax.optimization_barrier((chosen_rows, encoded))
    first_hidden, slope = hidden_of(encoded)
    picked = lax.all_to_all(chosen_rows, "feat", split_axis=0, concat_axis=0, tiled=True)
    picked, slope, first_hidden = lax.optimization_barrier((picked, slope, first_hidden))
    emb_delta = top_tower(picked, labels[:, 0], top_weight, score_vector)
    emb_delta, encoded_far = lax.optimization_barrier((emb_delta, encoded_far))
    returned = lax.all_to_all(emb_delta, "feat", split_axis=0, concat_axis=0, tiled=True)
    slots_back = lax.broadcasted_iota(jnp.int32, (slot_count, positions.shape[0]), 0)
    placer = (positions[None, :] == slots_back).astype(jnp.bfloat16)
    row_grads = jnp.dot(
        placer, returned.reshape(-1, emb_width), preferred_element_type=jnp.float32
    )
    row_delta = row_grads.astype(jnp.bfloat16)
    row_delta_far = lax.ppermute(row_delta, "samp", across)

    first_pre_far = jnp.dot(encoded_far, weight_first, preferred_element_type=jnp.float32)
    hidden_far, slope_far = lax.optimization_barrier(
        (
            jax.nn.silu(first_pre_far).astype(jnp.bfloat16),
            silu_slope(first_pre_far).astype(jnp.bfloat16),
        )
    )

    def delta_of(rows, factor):
        back = jnp.einsum("re,ke->rk", rows, weight_second, preferred_element_type=jnp.float32)
        return (back * factor.astype(jnp.float32)).astype(jnp.bfloat16)

    near = (encoded, first_hidden, row_delta, delta_of(row_delta, slope))
    far = (encoded_far, hidden_far, row_delta_far, delta_of(row_delta_far, slope_far))
    depth = hash_count // samp_count
    share = hidden_count // samp_count

    def first_part(group, at):
        columns = lax.dynamic_slice_in_dim(group[0], at * depth, depth, axis=1)
        return jnp.einsum("rh,rk->hk", columns, group[3], preferred_element_type=jnp.float32)

    def second_part(group, at):
        columns = lax.dynamic_slice_in_dim(group[1], at * share, share, axis=1)
        return jnp.einsum("rk,re->ke", columns, group[2], preferred_element_type=jnp.float32)

    firsts, seconds = [], []
    for step in range(1, half):
        target = (samp_at + 2 * step) % samp_count
        pairs = [(i, (i + 2 * step) % samp_count) for i in range(samp_count)]
        first_out = (first_part(near, target) + first_part(far, target)).astype(jnp.bfloat16)
        firsts.append(lax.ppermute(first_out, "samp", pairs))
        second_out = (second_part(near, target) + second_part(far, target)).astype(jnp.bfloat16)
        seconds.append(lax.ppermute(second_out, "samp", pairs))
    share_first = first_part(near, samp_at) + first_part(far, samp_at)
    share_second = second_part(near, samp_at) + second_part(far, samp_at)
    share_first, share_second = lax.optimization_barrier((share_first, share_second))
    for arrived in firsts:
        share_first = share_first + arrived.astype(jnp.float32)
    for arrived in seconds:
        share_second = share_second + arrived.astype(jnp.float32)
    return (row_grads[None], share_first[None], share_second[None])


def solution(mesh):
    return jax.shard_map(
        local,
        mesh=mesh,
        in_specs=(
            P("feat", "samp", None),
            P("feat", "samp"),
            P("feat", "samp"),
            P("feat", None, None),
            P("feat", None, None),
            P(),
            P(),
        ),
        out_specs=(P("feat", "samp", None), P("feat", "samp", None), P("feat", "samp", None)),
        check_vma=False,
    )
```
